32 devices in a mesh: group: 4 (over y, core), blk: 8 (over z, x).
Axes of the slice: x: 2, y: 2, z: 4, core: 2. Of those that a mesh axis runs over, the one named last changes fastest.
Arguments:
- queries: bfloat16 [2048, 32, 128], P('blk'), may hold values from -8 to 8
- doc_blocks: bfloat16 [4, 128, 128, 128], P('group', 'blk'), may hold values from -2 to 2
- doc_len: int32 [4, 128], P('group', 'blk'), may hold values from 96 to 128
- candidates: int32 [4, 8, 4, 8], P('group', 'blk'), may hold values from 0 to 17, as said below
- cand_count: int32 [4, 8, 4], P('group', 'blk'), may hold values from 2 to 8, as said below
- hot_owned: int32 [4, 8, 1], P('group', 'blk'), may hold values from 0 to 15
- hot_taken: int32 [4, 8, 2], P('group', 'blk'), may hold values from 0 to 7, as said below
Outputs:
- top_scores: float32 [2048, 16], P('blk')
The draws below stay inside these ranges and needn't reach their ends.
Inputs may be any that keep to these rules, and one draw needn't show every extreme that they name: `candidates`: slots below 16 name a device's own blocks, the others its hot copies; entries at or past the hop's count are ignored. `cand_count`: every query block has 8 live candidates at one or more of its hops. `hot_taken`: entries are hot pool indices of the same group; every pool entry is held by some device.
All inputs are finite; a program needn't handle non-finite values.
Results may differ from the reference program's by a relative error of at most 0.0003.
Values may be sent and summed in bfloat16 or wider, within the bound.
A program may use at most 64 MiB of HBM per device.

```python
import jax
import jax.numpy as jnp
from jax import lax

DIM = 128
QTOK = 32
ROWS = 128
QPB = 256
DBLK_DEV = 16
HOT_PUB = 1
HOT_DEV = 2
HOPS = 4
CAP = 8
TOPK = 16
GROUPS = 4
SHARDS = 8
QUERIES = 2048
DOCS_GROUP = 128
SLOTS = 18
POOL = 8


topic_count = 16


def topic_table(key):
    table_key = jax.random.fold_in(key, 101)
    return jnp.clip(jax.random.normal(table_key, (topic_count, DIM), jnp.float32), -3.0, 3.0)


def draw_queries(key, part):
    table = topic_table(key)
    key_noise = jax.random.fold_in(key, 1)
    key_pick = jax.random.fold_in(key, 2)
    picks = jax.random.randint(key_pick, (QUERIES, 2), 0, topic_count)
    mixture = jnp.take(table, picks[:, 0], axis=0) + jnp.take(table, picks[:, 1], axis=0)
    shape = (QUERIES, QTOK, DIM)
    noise = jnp.clip(jax.random.normal(key_noise, shape, jnp.float32), -6.0, 6.0)
    values = noise + 0.15 * mixture[:, None, :]
    return values.astype(jnp.bfloat16)


def draw_doc_blocks(key, part):
    table = topic_table(key)
    key_noise = jax.random.fold_in(key, 11)
    key_pick = jax.random.fold_in(key, 12)
    picks = jax.random.randint(key_pick, (GROUPS, DOCS_GROUP), 0, topic_count)
    topics = jnp.take(table, picks, axis=0)
    shape = (GROUPS, DOCS_GROUP, ROWS, DIM)
    noise = jnp.clip(jax.random.normal(key_noise, shape, jnp.float32), -6.0, 6.0) * DIM ** (-0.5)
    values = noise + 0.05 * topics[:, :, None, :]
    return values.astype(jnp.bfloat16)


def draw_candidates(key, part):
    key_own, key_hot, key_pick = jax.random.split(key, 3)
    out_shape = (GROUPS, SHARDS, HOPS, CAP)
    own_slots = jax.random.randint(key_own, out_shape, 0, DBLK_DEV)
    hot_slots = DBLK_DEV + jax.random.randint(key_hot, out_shape, 0, HOT_DEV)
    chooser = jax.random.randint(key_pick, out_shape, 0, 2)
    slots = jnp.where(chooser == 0, own_slots, hot_slots).astype(jnp.int32)
    slots = slots.at[0, 0, 0, 0].set(SLOTS - 1)
    slots = slots.at[0, 0, 0, 1].set(0)
    return slots


def draw_cand_count(key, part):
    key_count, key_full = jax.random.split(key, 2)
    lowest = max(1, CAP // 4)
    counts = jax.random.randint(key_count, (GROUPS, SHARDS, HOPS), lowest, CAP + 1)
    full_hop = jax.random.randint(key_full, (GROUPS, SHARDS, 1), 0, HOPS)
    hop_index = jnp.arange(HOPS, dtype=jnp.int32)[None, None, :]
    counts = jnp.where(hop_index == full_hop, CAP, counts)
    first_row = jnp.where(jnp.arange(HOPS, dtype=jnp.int32) == full_hop[0, 0, 0], CAP, lowest)
    counts = counts.at[0, 0].set(first_row)
    return counts.astype(jnp.int32)


def draw_hot_taken(key, part):

    def per_group(group_key):
        key_first, key_other = jax.random.split(group_key, 2)
        first_take = jax.random.permutation(key_first, POOL).astype(jnp.int32).reshape(SHARDS, HOT_PUB)
        other_take = jax.random.randint(key_other, (SHARDS, HOT_DEV - HOT_PUB), 0, POOL).astype(jnp.int32)
        return jnp.concatenate([first_take, other_take], axis=1)
    group_keys = jax.random.split(key, GROUPS)
    return jax.vmap(per_group)(group_keys).astype(jnp.int32)


def with_ends(drawn, stream_key, low, high):
    longest = drawn.shape.index(max(drawn.shape))
    spots = []
    for shift in (0, 1):
        where = [jax.random.randint(jax.random.fold_in(stream_key, axis), (), 0, length) for axis, length in enumerate(drawn.shape)]
        where[longest] = (where[longest] + shift) % drawn.shape[longest]
        spots.append(tuple(where))
    return drawn.at[spots[0]].set(low).at[spots[1]].set(high)


def setup_inputs(seed: int = 0) -> dict:
    splits = jax.random.split(jax.random.key(seed), 8)
    queries = draw_queries(jax.random.fold_in(splits[7], 71), 0)
    doc_blocks = draw_doc_blocks(jax.random.fold_in(splits[7], 71), 0)
    doc_len = with_ends(jax.random.randint(splits[2], (GROUPS, DOCS_GROUP), ROWS - ROWS // 4, ROWS + 1), jax.random.fold_in(splits[2], 1), ROWS - ROWS // 4, ROWS).astype(jnp.int32)
    candidates = draw_candidates(jax.random.fold_in(splits[7], 71), 0)
    cand_count = draw_cand_count(jax.random.fold_in(splits[7], 71), 0)
    hot_owned = with_ends(jax.random.randint(splits[5], (GROUPS, SHARDS, HOT_PUB), 0, DBLK_DEV), jax.random.fold_in(splits[5], 1), 0, DBLK_DEV - 1).astype(jnp.int32)
    hot_taken = draw_hot_taken(jax.random.fold_in(splits[7], 71), 0)
    return {"queries": queries, "doc_blocks": doc_blocks, "doc_len": doc_len, "candidates": candidates, "cand_count": cand_count, "hot_owned": hot_owned, "hot_taken": hot_taken}


MASKED_SCORE = -1.0e30


def maxsim(query_part, blocks, lengths):
    def single(element):
        doc_block, length = element
        scores = lax.dot_general(query_part, doc_block, (((1,), (1,)), ((), ())), preferred_element_type=jnp.float32)
        keep_mask = jnp.arange(doc_block.shape[0], dtype=jnp.int32) < length
        scores = jnp.where(keep_mask[None, :], scores, MASKED_SCORE)
        best_rows = jnp.max(scores, axis=1).reshape(-1, QTOK)
        return jnp.sum(best_rows, axis=1) / QTOK
    return lax.map(single, (blocks, lengths)).T


def reference(queries, doc_blocks, doc_len, candidates, cand_count, hot_owned, hot_taken):
    own_ids = jnp.arange(SHARDS, dtype=jnp.int32)[:, None] * DBLK_DEV + jnp.arange(DBLK_DEV, dtype=jnp.int32)[None, :]
    group_ids = jnp.arange(GROUPS, dtype=jnp.int32)[:, None, None]
    owner_dev = hot_taken // HOT_PUB
    member = hot_taken % HOT_PUB
    hot_ids = owner_dev * DBLK_DEV + hot_owned[group_ids, owner_dev, member]
    ext_ids = jnp.concatenate([jnp.broadcast_to(own_ids[None], (GROUPS, SHARDS, DBLK_DEV)), hot_ids], axis=2)
    visit_dev = (jnp.arange(SHARDS, dtype=jnp.int32)[:, None] + jnp.arange(HOPS, dtype=jnp.int32)[None, :]) % SHARDS
    group_ids4 = jnp.arange(GROUPS, dtype=jnp.int32)[:, None, None, None]
    block_ids = ext_ids[group_ids4, visit_dev[None, :, :, None], candidates]
    valid_mask = jnp.arange(CAP, dtype=jnp.int32)[None, None, None, :] < cand_count[..., None]
    block_ids = block_ids.reshape(GROUPS, SHARDS, HOPS * CAP).transpose(1, 0, 2)
    valid_mask = valid_mask.reshape(GROUPS, SHARDS, HOPS * CAP).transpose(1, 0, 2)
    query_sets = queries.reshape(SHARDS, QPB * QTOK, DIM)

    def per_block(element):
        query_part, id_set, valid_set = element
        group_parts = []
        for group_index in range(GROUPS):
            blocks = jnp.take(doc_blocks[group_index], id_set[group_index], axis=0)
            lengths = jnp.take(doc_len[group_index], id_set[group_index], axis=0)
            scores = maxsim(query_part, blocks, lengths)
            group_parts.append(jnp.where(valid_set[group_index][None, :], scores, MASKED_SCORE))
        return lax.top_k(jnp.concatenate(group_parts, axis=1), TOPK)[0]

    top_values = lax.map(per_block, (query_sets, block_ids, valid_mask))
    return top_values.reshape(QUERIES, TOPK)
```

```python
import functools

import jax
import jax.numpy as jnp
from jax import lax
from jax.experimental import pallas as pl
from jax.experimental.pallas import tpu as pltpu
from jax.sharding import PartitionSpec as P

TOPK = 16
MASKED_SCORE = -1e30
LANES = 128
SUB = 8


def merge_desc(seq):
    n = len(seq)
    if n == 1:
        return seq
    half = n // 2
    hi = [jnp.maximum(seq[i], seq[i + half]) for i in range(half)]
    lo = [jnp.minimum(seq[i], seq[i + half]) for i in range(half)]
    return merge_desc(hi) + merge_desc(lo)


def sort_desc(seq):
    n = len(seq)
    if n == 1:
        return seq
    return merge_desc(sort_desc(seq[: n // 2]) + sort_desc(seq[n // 2 :])[::-1])


def kernel(dims, meta_s, meta_v, q_ref, doc_ref, out_ref,
           meta_in, meta_in_s, fixed, hot, sendbuf, recv, cur, maxes, scores,
           m_send, m_recv, m_local, h_send, h_recv, d_send, d_recv, g_send, g_recv):
    shards, groups, hops, cap, per_dev, hot_pub, hot_dev, offs, at = dims
    me = lax.axis_index("blk")
    grp = lax.axis_index("group")

    def peer(o):
        return lax.rem(me + (o % shards), shards)

    def gpeer(o):
        return lax.rem(grp + o, groups)

    barrier = pltpu.get_barrier_semaphore()
    for o in range(1, shards):
        pl.semaphore_signal(barrier, inc=1, device_id={"blk": peer(o)},
                            device_id_type=pl.DeviceIdType.MESH)
    for o in range(1, groups):
        pl.semaphore_signal(barrier, inc=1, device_id={"group": gpeer(o)},
                            device_id_type=pl.DeviceIdType.MESH)

    rows, dim = doc_ref.shape[2], doc_ref.shape[3]
    row_id = lax.broadcasted_iota(jnp.int32, (rows, dim), 0)

    def fix(i, carry):
        length = meta_s[0, at["len"] + i]
        block = doc_ref[0, i].astype(jnp.float32)
        fixed[i] = jnp.where(row_id < length, block, block[0:1, :]).astype(fixed.dtype)
        return carry

    lax.fori_loop(0, per_dev, fix, 0, unroll=2)
    for m in range(hot_pub):
        hot[me * hot_pub + m] = fixed[meta_s[0, at["owned"] + m]]

    pl.semaphore_wait(barrier, shards + groups - 2)

    meta_copies = {}
    for o in offs:
        slot = offs.index((-o) % shards)
        meta_copies[o] = pltpu.make_async_remote_copy(
            src_ref=meta_v, dst_ref=meta_in.at[slot], send_sem=m_send.at[slot],
            recv_sem=m_recv.at[slot], device_id={"blk": peer(o)},
            device_id_type=pl.DeviceIdType.MESH)
        meta_copies[o].start()
    hot_copies = []
    for o in range(1, shards):
        part = hot.at[pl.ds(me * hot_pub, hot_pub)]
        c = pltpu.make_async_remote_copy(
            src_ref=part, dst_ref=part, send_sem=h_send.at[o - 1],
            recv_sem=h_recv.at[o - 1], device_id={"blk": peer(o)},
            device_id_type=pl.DeviceIdType.MESH)
        c.start()
        hot_copies.append(c)
    for o in offs:
        meta_copies[o].wait_recv()
    local = pltpu.make_async_copy(meta_in, meta_in_s, m_local)
    local.start()
    local.wait()

    doc_copies = []
    for h in range(1, hops):
        slot = offs.index((-h) % shards)
        for c in range(cap):
            want = meta_in_s[slot, 0, at["cand"] + h * cap + c]
            sendbuf[h - 1, c] = fixed[jnp.clip(want, 0, per_dev - 1)]
        d = pltpu.make_async_remote_copy(
            src_ref=sendbuf.at[h - 1], dst_ref=recv.at[h - 1], send_sem=d_send.at[h - 1],
            recv_sem=d_recv.at[h - 1], device_id={"blk": peer(-h)},
            device_id_type=pl.DeviceIdType.MESH)
        d.start()
        doc_copies.append(d)

    for c in hot_copies:
        c.wait_recv()

    segs, tiles, qtok = q_ref.shape[0], q_ref.shape[1], q_ref.shape[2]
    width = segs * qtok
    lane = lax.broadcasted_iota(jnp.int32, (cap, LANES), 1)
    cand_id = lax.broadcasted_iota(jnp.int32, (cap, width), 0)
    for h in range(hops):
        if h > 0:
            doc_copies[h - 1].wait_recv()
        for c in range(cap):
            slot_id = meta_s[0, at["cand"] + h * cap + c]
            kth = jnp.clip(slot_id - per_dev, 0, hot_dev - 1)
            if h == 0:
                entry = meta_s[0, at["taken"] + kth]
                own = fixed[jnp.clip(slot_id, 0, per_dev - 1)]
            else:
                entry = meta_in_s[offs.index(h % shards), 0, at["taken"] + kth]
                own = recv[h - 1, c]
            hot_block = hot[jnp.clip(entry, 0, shards * hot_pub - 1)]
            cur[pl.ds(c * rows, rows), :] = jnp.where(slot_id >= per_dev, hot_block, own)

        def tile_step(j, carry):
            w = q_ref[:, j].reshape(width, dim)
            s = lax.dot_general(cur[...], w, (((1,), (1,)), ((), ())),
                                preferred_element_type=jnp.float32)
            maxes[j] = jnp.max(s.reshape(cap, rows, width), axis=1)
            return carry

        lax.fori_loop(0, tiles, tile_step, 0)

        halves = []
        for half in range(width // LANES):
            acc = jnp.zeros((cap, LANES), jnp.float32)
            for j in range(tiles):
                x = maxes[j, :, half * LANES : (half + 1) * LANES]
                step = qtok // 2
                while step:
                    x = x + pltpu.roll(x, step, 1)
                    step //= 2
                x = pltpu.roll(x, (j + 1 - qtok) % LANES, 1)
                acc = jnp.where(lane % qtok == j, x, acc)
            halves.append(acc * (1.0 / qtok))
        result = jnp.concatenate(halves, axis=1)
        live = meta_s[0, at["count"] + h]
        scores[grp, pl.ds(h * cap, cap), :] = jnp.where(cand_id < live, result, MASKED_SCORE)

    g_copies = []
    for o in range(1, groups):
        c = pltpu.make_async_remote_copy(
            src_ref=scores.at[grp], dst_ref=scores.at[grp], send_sem=g_send.at[o - 1],
            recv_sem=g_recv.at[o - 1], device_id={"group": gpeer(o)},
            device_id_type=pl.DeviceIdType.MESH)
        c.start()
        g_copies.append(c)
    for c in g_copies:
        c.wait_recv()

    for half in range(width // LANES):
        cols = slice(half * LANES, (half + 1) * LANES)
        seq = [scores[g, r : r + SUB, cols] for g in range(groups)
               for r in range(0, hops * cap, SUB)]
        seq = sort_desc(seq)[:TOPK]
        shift = SUB // 2
        while shift:
            other = [pltpu.roll(v, shift, 0) for v in seq]
            n = len(seq)
            seq = merge_desc([jnp.maximum(seq[i], other[n - 1 - i]) for i in range(n)])
            shift //= 2
        out_ref[:, cols] = jnp.concatenate([v[0:1, :] for v in seq], axis=0)

    for c in list(meta_copies.values()) + hot_copies + doc_copies + g_copies:
        c.wait_send()


def on_device(shards, groups, queries, doc_blocks, doc_len, candidates, cand_count,
              hot_owned, hot_taken):
    per_dev, rows, dim = doc_blocks.shape[1:]
    hops, cap = candidates.shape[2:]
    hot_pub, hot_dev = hot_owned.shape[2], hot_taken.shape[2]
    qpb, qtok = queries.shape[0], queries.shape[1]
    fields = (("cand", candidates), ("taken", hot_taken), ("owned", hot_owned),
              ("len", doc_len), ("count", cand_count))
    at, pos = {}, 0
    for name, arr in fields:
        at[name] = pos
        pos += arr.size
    flat = jnp.concatenate([a.reshape(-1) for _, a in fields])
    meta = jnp.pad(flat, (0, SUB * LANES - pos)).reshape(SUB, LANES)
    tiles = qtok
    segs = qpb // tiles
    q4 = queries.reshape(segs, tiles, qtok, dim)
    offs = sorted({o % shards for h in range(1, hops) for o in (h, -h)})
    dims = (shards, groups, hops, cap, per_dev, hot_pub, hot_dev, offs, at)
    vmem = pl.BlockSpec(memory_space=pltpu.VMEM)
    dma = pltpu.SemaphoreType.DMA
    bf = doc_blocks.dtype
    top = pl.pallas_call(
        functools.partial(kernel, dims),
        out_shape=jax.ShapeDtypeStruct((TOPK, qpb), jnp.float32),
        in_specs=[pl.BlockSpec(memory_space=pltpu.SMEM), vmem, vmem, vmem],
        out_specs=vmem,
        scratch_shapes=[
            pltpu.VMEM((len(offs), SUB, LANES), jnp.int32),
            pltpu.SMEM((len(offs), SUB, LANES), jnp.int32),
            pltpu.VMEM((per_dev, rows, dim), bf),
            pltpu.VMEM((shards * hot_pub, rows, dim), bf),
            pltpu.VMEM((hops - 1, cap, rows, dim), bf),
            pltpu.VMEM((hops - 1, cap, rows, dim), bf),
            pltpu.VMEM((cap * rows, dim), bf),
            pltpu.VMEM((tiles, cap, segs * qtok), jnp.float32),
            pltpu.VMEM((groups, hops * cap, qpb), jnp.float32),
            dma((len(offs),)), dma((len(offs),)), dma(()),
            dma((shards - 1,)), dma((shards - 1,)),
            dma((hops - 1,)), dma((hops - 1,)),
            dma((groups - 1,)), dma((groups - 1,)),
        ],
        compiler_params=pltpu.CompilerParams(
            collective_id=0, has_side_effects=True, vmem_limit_bytes=48 * 1024 * 1024),
    )(meta, meta, q4, doc_blocks)
    return top.T


def solution(mesh):
    return jax.shard_map(
        functools.partial(on_device, mesh.shape["blk"], mesh.shape["group"]),
        mesh=mesh,
        in_specs=(
            P("blk", None, None),
            P("group", "blk", None, None),
            P("group", "blk"),
            P("group", "blk", None, None),
            P("group", "blk", None),
            P("group", "blk", None),
            P("group", "blk", None),
        ),
        out_specs=P("blk", None),
        check_vma=False,
    )
```

```python
import functools

import jax
import jax.numpy as jnp
from jax import lax
from jax.experimental import pallas as pl
from jax.experimental.pallas import tpu as pltpu
from jax.sharding import PartitionSpec as P

TOPK = 16
MASKED_SCORE = -1e30
LANES = 128
UNROLL = 16
SUB = 8


def merge_desc(seq):
    n = len(seq)
    if n == 1:
        return seq
    half = n // 2
    hi = [jnp.maximum(seq[i], seq[i + half]) for i in range(half)]
    lo = [jnp.minimum(seq[i], seq[i + half]) for i in range(half)]
    return merge_desc(hi) + merge_desc(lo)


def sort_desc(seq):
    n = len(seq)
    if n == 1:
        return seq
    return merge_desc(sort_desc(seq[: n // 2]) + sort_desc(seq[n // 2 :])[::-1])


def kernel(dims, len_s, cand_s, count_s, owned_s, taken_s, cand_v, taken_v, q_hbm, doc_hbm,
           out_ref, q_ref, doc_ref, load_sem, meta_v, meta_in, meta_in_s, fixed, hot, sendbuf, recv, cur, maxes, scores,
           m_send, m_recv, m_local, h_send, h_recv, d_send, d_recv, g_send, g_recv):
    shards, groups, hops, cap, per_dev, hot_pub, hot_dev, offs = dims
    me = lax.axis_index("blk")
    grp = lax.axis_index("group")

    def peer(o):
        return lax.rem(me + (o % shards), shards)

    def gpeer(o):
        return lax.rem(grp + o, groups)

    barrier = pltpu.get_barrier_semaphore()
    for o in range(1, shards):
        pl.semaphore_signal(barrier, inc=1, device_id={"blk": peer(o)},
                            device_id_type=pl.DeviceIdType.MESH)
    for o in range(1, groups):
        pl.semaphore_signal(barrier, inc=1, device_id={"group": gpeer(o)},
                            device_id_type=pl.DeviceIdType.MESH)

    q_load = pltpu.make_async_copy(q_hbm, q_ref, load_sem.at[0])
    doc_load = pltpu.make_async_copy(doc_hbm, doc_ref, load_sem.at[1])
    doc_load.start()
    q_load.start()
    meta_v[...] = jnp.zeros_like(meta_v)
    meta_v[0:hops, 0:cap] = cand_v[0, 0]
    meta_v[hops : hops + 1, 0:hot_dev] = taken_v[0]
    doc_load.wait()

    rows, dim = doc_ref.shape[2], doc_ref.shape[3]
    row_id = lax.broadcasted_iota(jnp.int32, (rows, dim), 0)

    def fix(i, carry):
        length = len_s[0, i]
        block = doc_ref[0, i].astype(jnp.float32)
        fixed[i] = jnp.where(row_id < length, block, block[0:1, :]).astype(fixed.dtype)
        return carry

    lax.fori_loop(0, per_dev, fix, 0, unroll=2)
    for m in range(hot_pub):
        hot[me * hot_pub + m] = fixed[owned_s[0, 0, m]]

    pl.semaphore_wait(barrier, shards + groups - 2)

    meta_copies = {}
    for o in offs:
        slot = offs.index((-o) % shards)
        meta_copies[o] = pltpu.make_async_remote_copy(
            src_ref=meta_v, dst_ref=meta_in.at[slot], send_sem=m_send.at[slot],
            recv_sem=m_recv.at[slot], device_id={"blk": peer(o)},
            device_id_type=pl.DeviceIdType.MESH)
        meta_copies[o].start()
    hot_copies = []
    for o in range(1, shards):
        part = hot.at[pl.ds(me * hot_pub, hot_pub)]
        c = pltpu.make_async_remote_copy(
            src_ref=part, dst_ref=part, send_sem=h_send.at[o - 1],
            recv_sem=h_recv.at[o - 1], device_id={"blk": peer(o)},
            device_id_type=pl.DeviceIdType.MESH)
        c.start()
        hot_copies.append(c)
    for o in offs:
        meta_copies[o].wait_recv()
    local = pltpu.make_async_copy(meta_in, meta_in_s, m_local)
    local.start()
    local.wait()

    doc_copies = []
    for h in range(1, hops):
        slot = offs.index((-h) % shards)
        for c in range(cap):
            want = meta_in_s[slot, h, c]
            sendbuf[h - 1, c] = fixed[jnp.clip(want, 0, per_dev - 1)]
        d = pltpu.make_async_remote_copy(
            src_ref=sendbuf.at[h - 1], dst_ref=recv.at[h - 1], send_sem=d_send.at[h - 1],
            recv_sem=d_recv.at[h - 1], device_id={"blk": peer(-h)},
            device_id_type=pl.DeviceIdType.MESH)
        doc_copies.append(d)
        if h == 1:
            d.start()

    for c in hot_copies:
        c.wait_recv()
    q_load.wait()

    segs, tiles, qtok = q_ref.shape[0], q_ref.shape[1], q_ref.shape[2]
    width = segs * qtok
    lane = lax.broadcasted_iota(jnp.int32, (cap, LANES), 1)
    cand_id = lax.broadcasted_iota(jnp.int32, (cap, width), 0)
    for h in range(hops):
        if h > 0:
            doc_copies[h - 1].wait_recv()
        for c in range(cap):
            slot_id = cand_s[0, 0, h, c]
            kth = jnp.clip(slot_id - per_dev, 0, hot_dev - 1)
            if h == 0:
                entry = taken_s[0, 0, kth]
                own = fixed[jnp.clip(slot_id, 0, per_dev - 1)]
            else:
                entry = meta_in_s[offs.index(h % shards), hops, kth]
                own = recv[h - 1, c]
            hot_block = hot[jnp.clip(entry, 0, shards * hot_pub - 1)]
            cur[pl.ds(c * rows, rows), :] = jnp.where(slot_id >= per_dev, hot_block, own)

        def tile_step(j, carry):
            w = q_ref[:, j].reshape(width, dim)
            s = lax.dot_general(cur[...], w, (((1,), (1,)), ((), ())),
                                preferred_element_type=jnp.float32)
            maxes[j] = jnp.max(s.reshape(cap, rows, width), axis=1)
            return carry

        for part in range(2):
            lax.fori_loop(part * tiles // 2, (part + 1) * tiles // 2, tile_step, 0,
                          unroll=UNROLL)
            begin = part + 2
            if h == 0 and begin < hops:
                doc_copies[begin - 1].start()
        for begin in range(4, hops if h == 0 else 0):
            doc_copies[begin - 1].start()

        halves = []
        for half in range(width // LANES):
            acc = jnp.zeros((cap, LANES), jnp.float32)
            for j in range(tiles):
                x = maxes[j, :, half * LANES : (half + 1) * LANES]
                step = qtok // 2
                while step:
                    x = x + pltpu.roll(x, step, 1)
                    step //= 2
                x = pltpu.roll(x, (j + 1 - qtok) % LANES, 1)
                acc = jnp.where(lane % qtok == j, x, acc)
            halves.append(acc * (1.0 / qtok))
        result = jnp.concatenate(halves, axis=1)
        live = count_s[0, 0, h]
        scores[grp, pl.ds(h * cap, cap), :] = jnp.where(cand_id < live, result, MASKED_SCORE)

    g_copies = []
    for o in range(1, groups):
        c = pltpu.make_async_remote_copy(
            src_ref=scores.at[grp], dst_ref=scores.at[grp], send_sem=g_send.at[o - 1],
            recv_sem=g_recv.at[o - 1], device_id={"group": gpeer(o)},
            device_id_type=pl.DeviceIdType.MESH)
        c.start()
        g_copies.append(c)
    for c in g_copies:
        c.wait_recv()

    for half in range(width // LANES):
        cols = slice(half * LANES, (half + 1) * LANES)
        seq = [scores[g, r : r + SUB, cols] for g in range(groups)
               for r in range(0, hops * cap, SUB)]
        seq = sort_desc(seq)[:TOPK]
        shift = SUB // 2
        while shift:
            other = [pltpu.roll(v, shift, 0) for v in seq]
            n = len(seq)
            seq = merge_desc([jnp.maximum(seq[i], other[n - 1 - i]) for i in range(n)])
            shift //= 2
        out_ref[:, cols] = jnp.concatenate([v[0:1, :] for v in seq], axis=0)

    for c in list(meta_copies.values()) + hot_copies + doc_copies + g_copies:
        c.wait_send()


def on_device(shards, groups, queries, doc_blocks, doc_len, candidates, cand_count,
              hot_owned, hot_taken):
    per_dev, rows, dim = doc_blocks.shape[1:]
    hops, cap = candidates.shape[2:]
    hot_pub, hot_dev = hot_owned.shape[2], hot_taken.shape[2]
    qpb, qtok = queries.shape[0], queries.shape[1]
    tiles = qtok
    segs = qpb // tiles
    q4 = queries.reshape(segs, tiles, qtok, dim)
    offs = sorted({o % shards for h in range(1, hops) for o in (h, -h)})
    dims = (shards, groups, hops, cap, per_dev, hot_pub, hot_dev, offs)
    vmem = pl.BlockSpec(memory_space=pltpu.VMEM)
    anym = pl.BlockSpec(memory_space=pl.ANY)
    dma = pltpu.SemaphoreType.DMA
    bf = doc_blocks.dtype
    top = pl.pallas_call(
        functools.partial(kernel, dims),
        out_shape=jax.ShapeDtypeStruct((TOPK, qpb), jnp.float32),
        in_specs=[pl.BlockSpec(memory_space=pltpu.SMEM)] * 5 + [vmem] * 2 + [anym] * 2,
        out_specs=vmem,
        scratch_shapes=[
            pltpu.VMEM(q4.shape, bf),
            pltpu.VMEM(doc_blocks.shape, bf),
            dma((2,)),
            pltpu.VMEM((SUB, LANES), jnp.int32),
            pltpu.VMEM((len(offs), SUB, LANES), jnp.int32),
            pltpu.SMEM((len(offs), SUB, LANES), jnp.int32),
            pltpu.VMEM((per_dev, rows, dim), bf),
            pltpu.VMEM((shards * hot_pub, rows, dim), bf),
            pltpu.VMEM((hops - 1, cap, rows, dim), bf),
            pltpu.VMEM((hops - 1, cap, rows, dim), bf),
            pltpu.VMEM((cap * rows, dim), bf),
            pltpu.VMEM((tiles, cap, segs * qtok), jnp.float32),
            pltpu.VMEM((groups, hops * cap, qpb), jnp.float32),
            dma((len(offs),)), dma((len(offs),)), dma(()),
            dma((shards - 1,)), dma((shards - 1,)),
            dma((hops - 1,)), dma((hops - 1,)),
            dma((groups - 1,)), dma((groups - 1,)),
        ],
        compiler_params=pltpu.CompilerParams(
            collective_id=0, has_side_effects=True, vmem_limit_bytes=48 * 1024 * 1024),
    )(doc_len, candidates, cand_count, hot_owned, hot_taken, candidates, hot_taken,
      q4, doc_blocks)
    return top.T


def solution(mesh):
    return jax.shard_map(
        functools.partial(on_device, mesh.shape["blk"], mesh.shape["group"]),
        mesh=mesh,
        in_specs=(
            P("blk", None, None),
            P("group", "blk", None, None),
            P("group", "blk"),
            P("group", "blk", None, None),
            P("group", "blk", None),
            P("group", "blk", None),
            P("group", "blk", None),
        ),
        out_specs=P("blk", None),
        check_vma=False,
    )
```

```python
import functools

import jax
import jax.numpy as jnp
from jax import lax
from jax.experimental import pallas as pl
from jax.experimental.pallas import tpu as pltpu
from jax.sharding import PartitionSpec as P

TOPK = 16
MASKED_SCORE = -1e30
LANES = 128
SUB = 8


def merge_desc(seq):
    n = len(seq)
    if n == 1:
        return seq
    half = n // 2
    hi = [jnp.maximum(seq[i], seq[i + half]) for i in range(half)]
    lo = [jnp.minimum(seq[i], seq[i + half]) for i in range(half)]
    return merge_desc(hi) + merge_desc(lo)


def sort_desc(seq):
    n = len(seq)
    if n == 1:
        return seq
    return merge_desc(sort_desc(seq[: n // 2]) + sort_desc(seq[n // 2 :])[::-1])


def kernel(dims, len_s, cand_s, count_s, owned_s, taken_s, cand_v, taken_v, q_hbm, doc_hbm,
           out_ref, q_ref, doc_ref, load_sem, meta_v, meta_in, meta_in_s, fixed, hot, sendbuf, recv, cur, maxes, scores,
           m_send, m_recv, m_local, h_send, h_recv, d_send, d_recv, g_send, g_recv,
           r_send, r_recv, relay):
    shards, groups, hops, cap, per_dev, hot_pub, hot_dev, offs = dims
    me = lax.axis_index("blk")
    grp = lax.axis_index("group")

    def peer(o):
        return lax.rem(me + (o % shards), shards)

    def gpeer(o):
        return lax.rem(grp + o, groups)

    barrier = pltpu.get_barrier_semaphore()
    for o in range(1, shards):
        pl.semaphore_signal(barrier, inc=1, device_id={"blk": peer(o)},
                            device_id_type=pl.DeviceIdType.MESH)
    for o in range(1, groups):
        pl.semaphore_signal(barrier, inc=1, device_id={"group": gpeer(o)},
                            device_id_type=pl.DeviceIdType.MESH)

    q_load = pltpu.make_async_copy(q_hbm, q_ref, load_sem.at[0])
    doc_load = pltpu.make_async_copy(doc_hbm, doc_ref, load_sem.at[1])
    doc_load.start()
    q_load.start()
    meta_v[...] = jnp.zeros_like(meta_v)
    meta_v[0:hops, 0:cap] = cand_v[0, 0]
    meta_v[hops : hops + 1, 0:hot_dev] = taken_v[0]
    doc_load.wait()

    rows, dim = doc_ref.shape[2], doc_ref.shape[3]
    row_id = lax.broadcasted_iota(jnp.int32, (rows, dim), 0)

    def fix(i, carry):
        length = len_s[0, i]
        block = doc_ref[0, i].astype(jnp.float32)
        fixed[i] = jnp.where(row_id < length, block, block[0:1, :]).astype(fixed.dtype)
        return carry

    lax.fori_loop(0, per_dev, fix, 0, unroll=2)
    for m in range(hot_pub):
        hot[me * hot_pub + m] = fixed[owned_s[0, 0, m]]

    pl.semaphore_wait(barrier, shards + groups - 2)

    meta_copies = {}
    for o in offs:
        slot = offs.index((-o) % shards)
        meta_copies[o] = pltpu.make_async_remote_copy(
            src_ref=meta_v, dst_ref=meta_in.at[slot], send_sem=m_send.at[slot],
            recv_sem=m_recv.at[slot], device_id={"blk": peer(o)},
            device_id_type=pl.DeviceIdType.MESH)
        meta_copies[o].start()
    hot_copies = []
    for o in range(1, shards):
        part = hot.at[pl.ds(me * hot_pub, hot_pub)]
        c = pltpu.make_async_remote_copy(
            src_ref=part, dst_ref=part, send_sem=h_send.at[o - 1],
            recv_sem=h_recv.at[o - 1], device_id={"blk": peer(o)},
            device_id_type=pl.DeviceIdType.MESH)
        c.start()
        hot_copies.append(c)
    for o in offs:
        meta_copies[o].wait_recv()
    local = pltpu.make_async_copy(meta_in, meta_in_s, m_local)
    local.start()
    local.wait()

    doc_copies = []
    for h in range(1, hops):
        slot = offs.index((-h) % shards)
        for c in range(cap):
            want = meta_in_s[slot, h, c]
            sendbuf[h - 1, c] = fixed[jnp.clip(want, 0, per_dev - 1)]
        d = pltpu.make_async_remote_copy(
            src_ref=sendbuf.at[h - 1], dst_ref=recv.at[h - 1], send_sem=d_send.at[h - 1],
            recv_sem=d_recv.at[h - 1], device_id={"blk": peer(-h)},
            device_id_type=pl.DeviceIdType.MESH)
        doc_copies.append(d)
    far = hops - 1
    relayed = far % 2 == 1 and far > 1 and shards % 2 == 0 and cap % 2 == 0
    part_a = pl.ds(0, cap // 2)
    part_b = pl.ds(cap // 2, cap // 2)
    even = lax.rem(me, 2) == 0
    if relayed:
        def piece(src, dst, i, to):
            return pltpu.make_async_remote_copy(
                src_ref=src, dst_ref=dst, send_sem=r_send.at[i], recv_sem=r_recv.at[i],
                device_id={"blk": peer(to)}, device_id_type=pl.DeviceIdType.MESH)

        doc_copies[far - 1] = piece(sendbuf.at[far - 1, part_a], recv.at[far - 1, part_a], 0, -far)
        straight = piece(sendbuf.at[far - 1, part_b], recv.at[far - 1, part_b], 1, -far)
        first_leg = piece(sendbuf.at[far - 1, part_b], relay, 2, -far - 1)
        last_leg = piece(relay, recv.at[far - 1, part_b], 1, 1)

        @pl.when(even)
        def _():
            first_leg.start()

        @pl.when(jnp.logical_not(even))
        def _():
            straight.start()

    for d in doc_copies:
        d.start()

    for c in hot_copies:
        c.wait_recv()
    q_load.wait()

    segs, tiles, qtok = q_ref.shape[0], q_ref.shape[1], q_ref.shape[2]
    width = segs * qtok
    lane = lax.broadcasted_iota(jnp.int32, (cap, LANES), 1)
    cand_id = lax.broadcasted_iota(jnp.int32, (cap, width), 0)
    for h in range(hops):
        if h > 0:
            doc_copies[h - 1].wait_recv()
            if relayed and h == far:
                straight.wait_recv()
        for c in range(cap):
            slot_id = cand_s[0, 0, h, c]
            kth = jnp.clip(slot_id - per_dev, 0, hot_dev - 1)
            if h == 0:
                entry = taken_s[0, 0, kth]
                own = fixed[jnp.clip(slot_id, 0, per_dev - 1)]
            else:
                entry = meta_in_s[offs.index(h % shards), hops, kth]
                own = recv[h - 1, c]
            hot_block = hot[jnp.clip(entry, 0, shards * hot_pub - 1)]
            cur[pl.ds(c * rows, rows), :] = jnp.where(slot_id >= per_dev, hot_block, own)

        def tile_step(j, carry):
            w = q_ref[:, j].reshape(width, dim)
            s = lax.dot_general(cur[...], w, (((1,), (1,)), ((), ())),
                                preferred_element_type=jnp.float32)
            maxes[j] = jnp.max(s.reshape(cap, rows, width), axis=1)
            return carry

        parts = 2 if h == 0 else 1
        for part in range(parts):
            lax.fori_loop(part * tiles // parts, (part + 1) * tiles // parts, tile_step, 0,
                          unroll=tiles // parts)
        if h == 0 and relayed:
            @pl.when(even)
            def _():
                first_leg.wait_recv()
                last_leg.start()

        halves = []
        for half in range(width // LANES):
            acc = jnp.zeros((cap, LANES), jnp.float32)
            for j in range(tiles):
                x = maxes[j, :, half * LANES : (half + 1) * LANES]
                step = qtok // 2
                while step:
                    x = x + pltpu.roll(x, step, 1)
                    step //= 2
                x = pltpu.roll(x, (j + 1 - qtok) % LANES, 1)
                acc = jnp.where(lane % qtok == j, x, acc)
            halves.append(acc * (1.0 / qtok))
        result = jnp.concatenate(halves, axis=1)
        live = count_s[0, 0, h]
        scores[grp, pl.ds(h * cap, cap), :] = jnp.where(cand_id < live, result, MASKED_SCORE)

    g_copies = []
    for o in range(1, groups):
        c = pltpu.make_async_remote_copy(
            src_ref=scores.at[grp], dst_ref=scores.at[grp], send_sem=g_send.at[o - 1],
            recv_sem=g_recv.at[o - 1], device_id={"group": gpeer(o)},
            device_id_type=pl.DeviceIdType.MESH)
        c.start()
        g_copies.append(c)
    for c in g_copies:
        c.wait_recv()

    for half in range(width // LANES):
        cols = slice(half * LANES, (half + 1) * LANES)
        seq = [scores[g, r : r + SUB, cols] for g in range(groups)
               for r in range(0, hops * cap, SUB)]
        seq = sort_desc(seq)[:TOPK]
        shift = SUB // 2
        while shift:
            other = [pltpu.roll(v, shift, 0) for v in seq]
            n = len(seq)
            seq = merge_desc([jnp.maximum(seq[i], other[n - 1 - i]) for i in range(n)])
            shift //= 2
        out_ref[:, cols] = jnp.concatenate([v[0:1, :] for v in seq], axis=0)

    if relayed:
        straight.wait_send()

        @pl.when(even)
        def _():
            first_leg.wait_send()

    for c in list(meta_copies.values()) + hot_copies + doc_copies + g_copies:
        c.wait_send()


def on_device(shards, groups, queries, doc_blocks, doc_len, candidates, cand_count,
              hot_owned, hot_taken):
    per_dev, rows, dim = doc_blocks.shape[1:]
    hops, cap = candidates.shape[2:]
    hot_pub, hot_dev = hot_owned.shape[2], hot_taken.shape[2]
    qpb, qtok = queries.shape[0], queries.shape[1]
    tiles = qtok
    segs = qpb // tiles
    q4 = queries.reshape(segs, tiles, qtok, dim)
    offs = sorted({o % shards for h in range(1, hops) for o in (h, -h)})
    dims = (shards, groups, hops, cap, per_dev, hot_pub, hot_dev, offs)
    vmem = pl.BlockSpec(memory_space=pltpu.VMEM)
    anym = pl.BlockSpec(memory_space=pl.ANY)
    dma = pltpu.SemaphoreType.DMA
    bf = doc_blocks.dtype
    top = pl.pallas_call(
        functools.partial(kernel, dims),
        out_shape=jax.ShapeDtypeStruct((TOPK, qpb), jnp.float32),
        in_specs=[pl.BlockSpec(memory_space=pltpu.SMEM)] * 5 + [vmem] * 2 + [anym] * 2,
        out_specs=vmem,
        scratch_shapes=[
            pltpu.VMEM(q4.shape, bf),
            pltpu.VMEM(doc_blocks.shape, bf),
            dma((2,)),
            pltpu.VMEM((SUB, LANES), jnp.int32),
            pltpu.VMEM((len(offs), SUB, LANES), jnp.int32),
            pltpu.SMEM((len(offs), SUB, LANES), jnp.int32),
            pltpu.VMEM((per_dev, rows, dim), bf),
            pltpu.VMEM((shards * hot_pub, rows, dim), bf),
            pltpu.VMEM((hops - 1, cap, rows, dim), bf),
            pltpu.VMEM((hops - 1, cap, rows, dim), bf),
            pltpu.VMEM((cap * rows, dim), bf),
            pltpu.VMEM((tiles, cap, segs * qtok), jnp.float32),
            pltpu.VMEM((groups, hops * cap, qpb), jnp.float32),
            dma((len(offs),)), dma((len(offs),)), dma(()),
            dma((shards - 1,)), dma((shards - 1,)),
            dma((hops - 1,)), dma((hops - 1,)),
            dma((groups - 1,)), dma((groups - 1,)),
            dma((3,)), dma((3,)),
            pltpu.VMEM((cap // 2, rows, dim), bf),
        ],
        compiler_params=pltpu.CompilerParams(
            collective_id=0, has_side_effects=True, vmem_limit_bytes=48 * 1024 * 1024),
    )(doc_len, candidates, cand_count, hot_owned, hot_taken, candidates, hot_taken,
      q4, doc_blocks)
    return top.T


def solution(mesh):
    return jax.shard_map(
        functools.partial(on_device, mesh.shape["blk"], mesh.shape["group"]),
        mesh=mesh,
        in_specs=(
            P("blk", None, None),
            P("group", "blk", None, None),
            P("group", "blk"),
            P("group", "blk", None, None),
            P("group", "blk", None),
            P("group", "blk", None),
            P("group", "blk", None),
        ),
        out_specs=P("blk", None),
        check_vma=False,
    )
```
